256 devices in a mesh: dp: 64 (over z_lo, x, y, core), mp: 4 (over z_hi).
Axes of the slice: x: 4, y: 4, z: 8 (z_hi: 4, z_lo: 2; z = z_hi * 2 + z_lo), core: 2. Of those that a mesh axis runs over, the one named last changes fastest.
Arguments:
- activations: bfloat16 [32768, 2560], P('dp', 'mp'), may hold values from -80 to 80
- output_grad: bfloat16 [32768, 2560], P(('dp', 'mp')), may hold values from -80 to 80
- act_inverse: bfloat16 [2560, 640], P('mp'), may hold values from -3 to 3
- grad_inverse: bfloat16 [2560, 640], replicated, may hold values from -3 to 3
Outputs:
- act_cov: float32 [2560, 640], P(('mp', 'dp'))
- grad_cov: float32 [2560, 640], P(('dp', 'mp'))
- update: bfloat16 [2560, 2560], P('mp')
The draws below stay inside these ranges and needn't reach their ends.
All inputs are finite; a program needn't handle non-finite values.
Results may differ from the reference program's by a relative error of at most 0.0046.
The reference program's roundings to bfloat16 on the way (of `left`) count: a program that leaves them out, or rounds other values in their place, can miss the bound.
Values may be sent and summed in bfloat16 or wider, within the bound.
No kernel may reach another device: no remote copies, remote signals or barrier semaphores. Data moves between devices by JAX's collectives and lax.ppermute only.
A program may use at most 128 MiB of HBM per device.

```python
import math
import jax
import jax.numpy as jnp
from jax import lax

DOUT = 2560
HID = 2560
BLK = 640
TOKENS = 32768


def block_matrix(values, diagonal, spread_scale):
    size = values.shape[1]
    symmetric = (values + jnp.swapaxes(values, 1, 2)) * (spread_scale / math.sqrt(size))
    index_rows = jnp.arange(size)[:, None]
    index_cols = jnp.arange(size)[None, :]
    identity_mask = (index_rows == index_cols).astype(jnp.float32)
    return symmetric + diagonal * identity_mask


def draw_activations(key, part):
    key = jax.random.fold_in(key, 11)
    key_values, key_cols, key_rows = jax.random.split(key, 3)
    rising = 0.6 + 0.6 * (jnp.arange(HID) % BLK).astype(jnp.float32) / BLK
    values = jnp.clip(jax.random.normal(key_values, (TOKENS, HID), jnp.float32), -5.0, 5.0)
    col_scale = jnp.exp(jax.random.uniform(key_cols, (1, HID), jnp.float32, math.log(0.3), math.log(3.0)))
    row_scale = jnp.exp(jax.random.uniform(key_rows, (TOKENS, 1), jnp.float32, math.log(0.4), math.log(4.0)))
    return (values * row_scale * col_scale * rising[None, :]).astype(jnp.bfloat16)


def draw_output_grad(key, part):
    key = jax.random.fold_in(key, 12)
    key_values, key_cols, key_rows = jax.random.split(key, 3)
    values = jnp.clip(jax.random.normal(key_values, (TOKENS, DOUT), jnp.float32), -5.0, 5.0)
    col_scale = jnp.exp(jax.random.uniform(key_cols, (1, DOUT), jnp.float32, math.log(0.3), math.log(3.0)))
    row_scale = jnp.exp(jax.random.uniform(key_rows, (TOKENS, 1), jnp.float32, math.log(0.4), math.log(4.0)))
    return (values * row_scale * col_scale * 1.2).astype(jnp.bfloat16)


def draw_act_inverse(key, part):
    key = jax.random.fold_in(key, 13)
    key_values, key_diag = jax.random.split(key, 2)
    block_count = HID // BLK
    values = jnp.clip(jax.random.normal(key_values, (block_count, BLK, BLK), jnp.float32), -4.0, 4.0)
    diagonal = jnp.exp(jax.random.uniform(key_diag, (block_count, BLK, 1), jnp.float32, math.log(0.5), math.log(2.0)))
    return block_matrix(values, diagonal, 0.35).reshape(HID, BLK).astype(jnp.bfloat16)


def draw_grad_inverse(key, part):
    key = jax.random.fold_in(key, 14)
    key_values, key_diag = jax.random.split(key, 2)
    block_count = DOUT // BLK
    values = jnp.clip(jax.random.normal(key_values, (block_count, BLK, BLK), jnp.float32), -4.0, 4.0)
    diagonal = jnp.exp(jax.random.uniform(key_diag, (block_count, BLK, 1), jnp.float32, math.log(0.5), math.log(2.0)))
    return block_matrix(values, diagonal, 0.35).reshape(DOUT, BLK).astype(jnp.bfloat16)


def setup_inputs(seed: int = 0) -> dict:
    key_list = jax.random.split(jax.random.key(seed), 5)
    activations = draw_activations(jax.random.fold_in(key_list[4], 71), 0)
    output_grad = draw_output_grad(jax.random.fold_in(key_list[4], 71), 0)
    act_inverse = draw_act_inverse(jax.random.fold_in(key_list[4], 71), 0)
    grad_inverse = draw_grad_inverse(jax.random.fold_in(key_list[4], 71), 0)
    return {"activations": activations, "output_grad": output_grad, "act_inverse": act_inverse, "grad_inverse": grad_inverse}


def reference(activations, output_grad, act_inverse, grad_inverse):
    inv_tokens = 1.0 / TOKENS
    act_blocks = []
    for block in range(HID // BLK):
        column_piece = activations[:, block * BLK:(block + 1) * BLK]
        act_blocks.append(jnp.dot(column_piece.T, column_piece, preferred_element_type=jnp.float32) * inv_tokens)
    act_cov = jnp.concatenate(act_blocks, axis=0)
    grad_blocks = []
    for block in range(DOUT // BLK):
        column_piece = output_grad[:, block * BLK:(block + 1) * BLK]
        grad_blocks.append(jnp.dot(column_piece.T, column_piece, preferred_element_type=jnp.float32) * inv_tokens)
    grad_cov = jnp.concatenate(grad_blocks, axis=0)
    weight_grad = jnp.dot(activations.T, output_grad, preferred_element_type=jnp.float32) * inv_tokens
    left_rows = []
    for block in range(HID // BLK):
        inverse_block = act_inverse[block * BLK:(block + 1) * BLK].astype(jnp.float32)
        grad_piece = weight_grad[block * BLK:(block + 1) * BLK]
        product = jnp.dot(inverse_block, grad_piece, precision=lax.Precision.HIGHEST)
        left_rows.append(product.astype(jnp.bfloat16))
    left = jnp.concatenate(left_rows, axis=0)
    right_cols = []
    for block in range(DOUT // BLK):
        right_cols.append(jnp.dot(left[:, block * BLK:(block + 1) * BLK], grad_inverse[block * BLK:(block + 1) * BLK], preferred_element_type=jnp.float32))
    precond = jnp.concatenate(right_cols, axis=1)
    mean_square = jnp.sum(precond * precond) / (HID * DOUT)
    update = (precond * lax.rsqrt(mean_square + 1e-06)).astype(jnp.bfloat16)
    return (act_cov, grad_cov, update)
```

```python
import jax
import jax.numpy as jnp
from jax import lax
from jax.sharding import Mesh, PartitionSpec as P

DP = ("zlo", "x", "y", "core")
EVERY = DP + ("zhi",)
PLANE = ("x", "y")
BF16 = jnp.bfloat16
F32 = jnp.float32


def shift(value, axis, step):
    count = lax.axis_size(axis)
    return lax.ppermute(value, axis, [(i, (i + step) % count) for i in range(count)])


def token_dot(lhs, rhs):
    return lax.dot_general(lhs, rhs, (((0,), (0,)), ((), ())), preferred_element_type=F32)


def spread_sum(partial, inv_tokens):
    peers = lax.axis_size("x") * lax.axis_size("y")
    rows = partial.shape[0] // peers
    sent = (partial * inv_tokens).astype(BF16).reshape(peers, rows, partial.shape[1])
    got = lax.all_to_all(sent, PLANE, split_axis=0, concat_axis=0, tiled=True)
    return jnp.sum(got.astype(F32), axis=0)


def plane_gather(piece):
    peers = lax.axis_size("x") * lax.axis_size("y")
    copies = jnp.broadcast_to(piece[None], (peers,) + piece.shape)
    got = lax.all_to_all(copies, PLANE, split_axis=0, concat_axis=0, tiled=True)
    return got.reshape(peers * piece.shape[0], piece.shape[1])


def body(activations, output_grad, act_inverse, grad_inverse):
    token_count, width = activations.shape
    out_width = output_grad.shape[1]
    dp_count = 1
    for name in DP:
        dp_count *= lax.axis_size(name)
    heads = lax.axis_size("zhi")
    group = token_count // heads
    half = out_width // 2
    inv_tokens = 1.0 / (token_count * dp_count)
    core = lax.axis_index("core")
    head = lax.axis_index("zhi")
    zlo = lax.axis_index("zlo")

    def swap_core(value):
        return shift(value, "core", 1)

    chunks = []
    for part in range(2):
        kept = lax.dynamic_slice_in_dim(output_grad, core * half + part * width, width, 1)
        given = lax.dynamic_slice_in_dim(output_grad, (1 - core) * half + part * width, width, 1)
        chunks.append(jnp.concatenate([kept, swap_core(given)], axis=0))
    other_act = swap_core(activations)

    offsets = (0, heads - 1, 1, 2)
    acts = []
    for offset in offsets:
        start = lax.rem(head + offset, heads) * group
        mine = lax.dynamic_slice_in_dim(activations, start, group, 0)
        theirs = lax.dynamic_slice_in_dim(other_act, start, group, 0)
        acts.append(jnp.concatenate([mine, theirs], axis=0))

    pieces = []
    for part, chunk in enumerate(chunks):
        ahead = shift(chunk, "zhi", 1)
        back = shift(chunk, "zhi", -1)
        far = shift(ahead, "zhi", 1) if part == 0 else shift(back, "zhi", -1)
        pieces.append((chunk, ahead, back, far))

    left_t = []
    for part in range(2):
        partial = sum(token_dot(piece, act) for piece, act in zip(pieces[part], acts))
        share = spread_sum(partial, inv_tokens)
        share = share + shift(share, "zlo", 1)
        mixed = lax.dot_general(
            share,
            act_inverse.astype(F32),
            (((1,), (1,)), ((), ())),
            precision=lax.Precision.HIGHEST,
        ).astype(BF16)
        mine = plane_gather(mixed)
        theirs = swap_core(mine)
        left_t.append((jnp.where(core == 0, mine, theirs), jnp.where(core == 0, theirs, mine)))
    blocks = [left_t[0][0], left_t[1][0], left_t[0][1], left_t[1][1]]

    does_grad = core == head // 2
    total = 0.0
    for index, act in enumerate(acts):
        grad_piece = jnp.where(head % 2 == 0, pieces[0][index], pieces[1][index])
        chosen = jnp.where(does_grad, grad_piece, act)
        total = total + token_dot(chosen, chosen)
    cov = spread_sum(total, inv_tokens)
    rows = cov.shape[0] // 2
    cov_kept = lax.dynamic_slice_in_dim(cov, zlo * rows, rows, 0)
    cov_given = lax.dynamic_slice_in_dim(cov, (1 - zlo) * rows, rows, 0)
    cov = cov_kept + shift(cov_given, "zlo", 1)
    rows = rows // 2
    cov_kept = lax.dynamic_slice_in_dim(cov, core * rows, rows, 0)
    cov_given = lax.dynamic_slice_in_dim(cov, (1 - core) * rows, rows, 0)
    cov_taken = swap_core(cov_given)
    act_rows = jnp.where(does_grad, cov_taken, cov_kept)
    grad_rows = jnp.where(does_grad, cov_kept, cov_taken)
    act_perm, grad_perm = [], []
    sites = lax.axis_size("x") * lax.axis_size("y")
    for zl in range(lax.axis_size("zlo")):
        for site in range(sites):
            for co in range(2):
                source = (zl * sites + site) * 2 + co
                place = (site * 2 + zl) * 2 + co
                act_perm.append((source, place))
                for hd in range(heads):
                    grad_perm.append((source * heads + hd, hd * dp_count + place))
    act_cov = lax.ppermute(act_rows, DP, act_perm)
    grad_cov = lax.ppermute(grad_rows, EVERY, grad_perm)

    results, squares = [], 0.0
    for index, block in enumerate(blocks):
        inverse = grad_inverse[index * width : (index + 1) * width]
        result = token_dot(block, inverse)
        squares = squares + jnp.sum(result * result)
        results.append(result)
    squares = jnp.broadcast_to(squares, (8, 128))
    total_sq = squares
    for step in range(1, heads):
        total_sq = total_sq + shift(squares, "zhi", step)
    mean_square = total_sq[0, 0] / (width * heads * out_width)
    precond = jnp.concatenate(results, axis=1)
    update = (precond * lax.rsqrt(mean_square + 1e-06)).astype(BF16)
    return (act_cov, grad_cov, update)


def solution(mesh):
    fine = Mesh(mesh.devices.reshape(2, 4, 4, 2, 4), EVERY)
    return jax.shard_map(
        body,
        mesh=fine,
        in_specs=(P(DP, "zhi"), P(EVERY, None), P("zhi", None), P()),
        out_specs=(P(("zhi",) + DP, None), P(EVERY, None), P("zhi", None)),
        check_vma=False,
    )
```

```python
import functools

import jax
import jax.numpy as jnp
from jax import lax
from jax.experimental import pallas as pl
from jax.experimental.pallas import tpu as pltpu
from jax.sharding import Mesh, PartitionSpec as P

DP = ("zlo", "x", "y", "core")
EVERY = DP + ("zhi",)
PLANE = ("x", "y")
BF16 = jnp.bfloat16
F32 = jnp.float32
LIMIT = pltpu.CompilerParams(vmem_limit_bytes=40 * 1024 * 1024)
VMEM = pl.BlockSpec(memory_space=pltpu.VMEM)
SMEM = pl.BlockSpec(memory_space=pltpu.SMEM)


def shift(value, axis, step):
    count = lax.axis_size(axis)
    return lax.ppermute(value, axis, [(i, (i + step) % count) for i in range(count)])


def after(value, *earlier):
    return lax.optimization_barrier((value,) + earlier)[0]


def token_dot(lhs, rhs):
    return lax.dot_general(lhs, rhs, (((0,), (0,)), ((), ())), preferred_element_type=F32)


def partial_kernel(scale, choice, *refs):
    first, second, acts, out = refs[:4], refs[4:8], refs[8:12], refs[12]
    sites, _, rows, _ = out.shape

    def product(lefts, rights):
        return sum(token_dot(left[...], right[...]) for left, right in zip(lefts, rights))

    cols = first[0].shape[1]
    for part, pieces in enumerate((first, second)):
        total = product(pieces, acts)
        for index in range(cols // rows):
            slab = part * (cols // rows) + index
            piece = total[index * rows : (index + 1) * rows] * scale
            out[slab // 2, slab % 2] = piece.astype(BF16)

    for which, pieces in enumerate((acts, first, second)):

        @pl.when(choice[0] == which)
        def _():
            total = product(pieces, pieces)
            for index in range(sites):
                piece = total[index * rows : (index + 1) * rows] * scale
                out[index, 2] = piece.astype(BF16)


def partial_sums(choice, pieces, acts, scale, sites):
    width = acts[0].shape[1]
    return pl.pallas_call(
        functools.partial(partial_kernel, scale),
        out_shape=jax.ShapeDtypeStruct((sites, 3, width // sites, width), BF16),
        in_specs=[SMEM] + [VMEM] * 12,
        out_specs=VMEM,
        compiler_params=LIMIT,
        cost_estimate=pl.CostEstimate(flops=6 * 1024 * width * width, bytes_accessed=8 * 2**20, transcendentals=0),
        name="partial_sums",
    )(choice, *pieces, *acts)


def right_kernel(mine, theirs, inv_mine, inv_theirs, out_mine, out_theirs, squares):
    width = mine.shape[1]
    for slot, (left, inverse, out) in enumerate(((mine, inv_mine, out_mine), (theirs, inv_theirs, out_theirs))):
        total = 0.0
        for part in range(2):
            rows = slice(part * width, (part + 1) * width)
            result = token_dot(left[rows, :], inverse[rows, :])
            out[part] = result
            total = total + jnp.sum(result * result)
        squares[slot] = jnp.broadcast_to(total, squares.shape[1:])


def right_product(mine, theirs, inv_mine, inv_theirs):
    width = mine.shape[1]
    block = jax.ShapeDtypeStruct((2, width, width), F32)
    return pl.pallas_call(
        right_kernel,
        out_shape=(block, block, jax.ShapeDtypeStruct((2, 8, 128), F32)),
        in_specs=[VMEM] * 4,
        out_specs=(VMEM, VMEM, VMEM),
        compiler_params=LIMIT,
        cost_estimate=pl.CostEstimate(flops=8 * width**3, bytes_accessed=12 * 2**20, transcendentals=0),
        name="right_product",
    )(mine, theirs, inv_mine, inv_theirs)


def final_kernel(count, core, own, sq_a, sq_b, sq_c, mine, theirs, out):
    total = own[...] + sq_a[...] + sq_b[...] + sq_c[...]
    scale = lax.rsqrt(total / count + 1e-06)[0:1, 0:1]
    width = mine.shape[2]

    def write(first, second):
        for index in range(4):
            block = (first, second)[index // 2][index % 2]
            out[:, index * width : (index + 1) * width] = (block * scale).astype(BF16)

    @pl.when(core[0] == 0)
    def _():
        write(mine, theirs)

    @pl.when(core[0] != 0)
    def _():
        write(theirs, mine)


def final_update(core, sums, blocks, count):
    width = blocks[0].shape[1]
    rows = width // 5
    small = pl.BlockSpec((8, 128), lambda i: (0, 0))
    tile = pl.BlockSpec((2, rows, width), lambda i: (0, i, 0))
    return pl.pallas_call(
        functools.partial(final_kernel, count),
        grid=(5,),
        out_shape=jax.ShapeDtypeStruct((width, 4 * width), BF16),
        in_specs=[SMEM] + [small] * 4 + [tile] * 2,
        out_specs=pl.BlockSpec((rows, 4 * width), lambda i: (i, 0)),
        compiler_params=LIMIT,
        cost_estimate=pl.CostEstimate(flops=4 * width * width, bytes_accessed=10 * 2**20, transcendentals=0),
        name="final_update",
    )(core, *sums, *blocks)


def plane_exchange(value):
    return lax.all_to_all(value, PLANE, split_axis=0, concat_axis=0, tiled=True)


def body(activations, output_grad, act_inverse, grad_inverse):
    token_count, width = activations.shape
    out_width = output_grad.shape[1]
    zlo_count = lax.axis_size("zlo")
    heads = lax.axis_size("zhi")
    sites = lax.axis_size("x") * lax.axis_size("y")
    dp_count = zlo_count * sites * 2
    group = token_count // heads
    half = out_width // 2
    rows = width // sites
    inv_tokens = 1.0 / (token_count * dp_count)
    core = lax.axis_index("core")
    head = lax.axis_index("zhi")
    zlo = lax.axis_index("zlo")

    def swap_core(value):
        return shift(value, "core", 1)

    chunks = []
    for part in range(2):
        kept = lax.dynamic_slice_in_dim(output_grad, core * half + part * width, width, 1)
        given = lax.dynamic_slice_in_dim(output_grad, (1 - core) * half + part * width, width, 1)
        chunks.append(jnp.concatenate([kept, swap_core(given)], axis=0))
    other_act = swap_core(activations)

    pieces = []
    for part, chunk in enumerate(chunks):
        ahead = shift(chunk, "zhi", 1)
        back = shift(chunk, "zhi", -1)
        far = shift(ahead, "zhi", 1) if part == 0 else shift(back, "zhi", -1)
        pieces += [chunk, ahead, back, far]

    acts = []
    for offset in (0, heads - 1, 1, 2):
        start = lax.rem(head + offset, heads) * group
        mine = lax.dynamic_slice_in_dim(activations, start, group, 0)
        theirs = lax.dynamic_slice_in_dim(other_act, start, group, 0)
        acts.append(jnp.concatenate([mine, theirs], axis=0))

    does_grad = core == head // 2
    choice = jnp.where(does_grad, 1 + head % 2, 0).astype(jnp.int32).reshape(1)
    partial = partial_sums(choice, pieces, acts, inv_tokens, sites)
    got = plane_exchange(partial)
    share = jnp.sum(got.astype(F32), axis=0)
    share = share + shift(share, "zlo", 1)

    mixed = lax.dot_general(
        share[:2].reshape(2 * rows, width),
        act_inverse.astype(F32),
        (((1,), (1,)), ((), ())),
        precision=lax.Precision.HIGHEST,
    ).astype(BF16)
    copies = jnp.broadcast_to(mixed.reshape(1, 2, rows, width), (sites, 2, rows, width))
    mine = plane_exchange(copies).reshape(half, width)

    cov = share[2].reshape(zlo_count, 2, rows // 4, width)
    cov = lax.dynamic_index_in_dim(cov, zlo, 0, False)
    kept = lax.dynamic_index_in_dim(cov, core, 0, False)
    taken = swap_core(lax.dynamic_index_in_dim(cov, 1 - core, 0, False))
    act_perm, grad_perm = [], []
    for zl in range(zlo_count):
        for site in range(sites):
            for co in range(2):
                source = (zl * sites + site) * 2 + co
                place = (site * zlo_count + zl) * 2 + co
                act_perm.append((source, place))
                for hd in range(heads):
                    grad_perm.append((source * heads + hd, hd * dp_count + place))
    act_cov = lax.ppermute(jnp.where(does_grad, taken, kept), DP, act_perm)
    grad_cov = lax.ppermute(jnp.where(does_grad, kept, taken), EVERY, grad_perm)

    mine = after(mine, act_cov, grad_cov)
    theirs = swap_core(mine)
    inv_mine = lax.dynamic_slice_in_dim(grad_inverse, core * half, half, 0)
    inv_theirs = lax.dynamic_slice_in_dim(grad_inverse, (1 - core) * half, half, 0)
    out_mine, out_theirs, squares = right_product(mine, theirs, inv_mine, inv_theirs)

    own_sq = squares[0] + squares[1]
    sums = [own_sq] + [shift(own_sq, "zhi", step) for step in range(1, heads)]
    count = width * heads * out_width
    update = final_update(core.astype(jnp.int32).reshape(1), sums, (out_mine, out_theirs), count)
    return (act_cov, grad_cov, update)


def solution(mesh):
    fine = Mesh(mesh.devices.reshape(2, 4, 4, 2, 4), EVERY)
    return jax.shard_map(
        body,
        mesh=fine,
        in_specs=(P(DP, "zhi"), P(EVERY, None), P("zhi", None), P()),
        out_specs=(P(("zhi",) + DP, None), P(EVERY, None), P("zhi", None)),
        check_vma=False,
    )
```

```python
import functools

import jax
import jax.numpy as jnp
from jax import lax
from jax.experimental import pallas as pl
from jax.experimental.pallas import tpu as pltpu
from jax.sharding import Mesh, PartitionSpec as P

DP = ("zlo", "x", "y", "core")
EVERY = DP + ("zhi",)
PLANE = ("x", "y")
BF16 = jnp.bfloat16
F32 = jnp.float32
LIMIT_MB = 16
LIMIT = pltpu.CompilerParams(vmem_limit_bytes=LIMIT_MB * 1024 * 1024)
VMEM = pl.BlockSpec(memory_space=pltpu.VMEM)
SMEM = pl.BlockSpec(memory_space=pltpu.SMEM)


def shift(value, axis, step):
    count = lax.axis_size(axis)
    return lax.ppermute(value, axis, [(i, (i + step) % count) for i in range(count)])


def after(value, *earlier):
    return lax.optimization_barrier((value,) + earlier)[0]


def token_dot(lhs, rhs):
    return lax.dot_general(lhs, rhs, (((0,), (0,)), ((), ())), preferred_element_type=F32)


def cost(flops, mib):
    return pl.CostEstimate(flops=flops, bytes_accessed=mib * 2**20, transcendentals=0)


def early_kernel(scale, *refs):
    pieces, acts, out = refs[:6], refs[6:9], refs[9]
    for part in range(2):
        total = sum(token_dot(pieces[3 * part + k][...], acts[k][...]) for k in range(3))
        out[part] = total * scale


def early_partial(pieces, acts, scale):
    width = acts[0].shape[1]
    return pl.pallas_call(
        functools.partial(early_kernel, scale),
        out_shape=jax.ShapeDtypeStruct((2, width, width), F32),
        in_specs=[VMEM] * 9,
        out_specs=VMEM,
        compiler_params=LIMIT,
        cost_estimate=cost(3 * 1024 * width * width, 6),
        name="early_partial",
    )(*pieces, *acts)


def weight_kernel(scale, early, first, second, act, out):
    rows = out.shape[1]
    for part, piece in enumerate((first, second)):
        total = early[part] + token_dot(piece[...], act[...]) * scale
        count = total.shape[0] // rows
        for index in range(count):
            out[part * count + index] = total[index * rows : (index + 1) * rows].astype(BF16)


def weight_partial(early, first, second, act, scale, sites):
    width = act.shape[1]
    return pl.pallas_call(
        functools.partial(weight_kernel, scale),
        out_shape=jax.ShapeDtypeStruct((sites, 2 * width // sites, width), BF16),
        in_specs=[VMEM] * 4,
        out_specs=VMEM,
        compiler_params=LIMIT,
        cost_estimate=cost(1024 * width * width, 6),
        name="weight_partial",
    )(early, first, second, act)


def cov_kernel(scale, first, second, acts, out):
    rows = out.shape[2]
    for slab, tokens in enumerate((first, second, acts)):
        value = tokens[...]
        total = token_dot(value, value)
        for index in range(out.shape[0]):
            out[index, slab] = (total[index * rows : (index + 1) * rows] * scale).astype(BF16)


def cov_partial(first, second, acts, scale, sites):
    width = acts.shape[1]
    return pl.pallas_call(
        functools.partial(cov_kernel, scale),
        out_shape=jax.ShapeDtypeStruct((sites, 3, width // sites, width), BF16),
        in_specs=[VMEM] * 3,
        out_specs=VMEM,
        compiler_params=LIMIT,
        cost_estimate=cost(2 * 1024 * width * width, 5),
        name="cov_partial",
    )(first, second, acts)


def right_kernel(half_index, left, inverse, out, squares):
    width = left.shape[1]
    total = 0.0
    for part in range(2):
        start = pl.multiple_of((2 * half_index[0] + part) * width, width)
        result = token_dot(left[part * width : (part + 1) * width, :], inverse[pl.ds(start, width), :])
        out[part] = result
        total = total + jnp.sum(result * result)
    squares[...] = jnp.broadcast_to(total, squares.shape)


def right_product(half_index, left, inverse):
    width = left.shape[1]
    return pl.pallas_call(
        right_kernel,
        out_shape=(jax.ShapeDtypeStruct((2, width, width), F32), jax.ShapeDtypeStruct((8, 128), F32)),
        in_specs=[SMEM, VMEM, VMEM],
        out_specs=(VMEM, VMEM),
        compiler_params=LIMIT,
        cost_estimate=cost(4 * width**3, 6),
        name="right_product",
    )(half_index, left, inverse)


def final_kernel(count, core, own, sq_a, sq_b, sq_c, act_rows, grad_rows, mine, theirs, out, act_out, grad_out):
    total = own[...] + sq_a[...] + sq_b[...] + sq_c[...]
    scale = lax.rsqrt(total / count + 1e-06)[0:1, 0:1]
    width = mine.shape[2]
    rows = out.shape[0]
    place = pl.ds(pl.multiple_of(pl.program_id(0) * rows, rows), rows)
    act_out[...] = act_rows[...]
    grad_out[...] = grad_rows[...]

    def write(first, second):
        for index in range(4):
            block = (first, second)[index // 2][index % 2, place]
            out[:, index * width : (index + 1) * width] = (block * scale).astype(BF16)

    @pl.when(core[0] == 0)
    def _():
        write(mine, theirs)

    @pl.when(core[0] != 0)
    def _():
        write(theirs, mine)


def final_update(core, sums, cov_rows, blocks, count):
    width = blocks[0].shape[1]
    rows = width // 5
    small = pl.BlockSpec((8, 128), lambda i: (0, 0))
    cov = pl.BlockSpec(cov_rows[0].shape, lambda i: (0, 0))
    cov_type = jax.ShapeDtypeStruct(cov_rows[0].shape, F32)
    return pl.pallas_call(
        functools.partial(final_kernel, count),
        grid=(5,),
        out_shape=(jax.ShapeDtypeStruct((width, 4 * width), BF16), cov_type, cov_type),
        in_specs=[SMEM] + [small] * 4 + [cov] * 2 + [VMEM] * 2,
        out_specs=(pl.BlockSpec((rows, 4 * width), lambda i: (i, 0)), cov, cov),
        compiler_params=LIMIT,
        cost_estimate=cost(4 * width * width, 10),
        name="final_update",
    )(core, *sums, *cov_rows, *blocks)


def plane_exchange(value):
    return lax.all_to_all(value, PLANE, split_axis=0, concat_axis=0, tiled=True)


def body(activations, output_grad, act_inverse, grad_inverse):
    token_count, width = activations.shape
    out_width = output_grad.shape[1]
    zlo_count = lax.axis_size("zlo")
    heads = lax.axis_size("zhi")
    sites = lax.axis_size("x") * lax.axis_size("y")
    dp_count = zlo_count * sites * 2
    group = token_count // heads
    half = out_width // 2
    rows = width // sites
    inv_tokens = 1.0 / (token_count * dp_count)
    core = lax.axis_index("core")
    head = lax.axis_index("zhi")

    def swap_core(value):
        return shift(value, "core", 1)

    chunks = []
    for part in range(2):
        kept = lax.dynamic_slice_in_dim(output_grad, core * half + part * width, width, 1)
        given = lax.dynamic_slice_in_dim(output_grad, (1 - core) * half + part * width, width, 1)
        chunks.append(jnp.concatenate([kept, swap_core(given)], axis=0))

    other_act = swap_core(activations)
    pieces = []
    for part, chunk in enumerate(chunks):
        ahead = shift(chunk, "zhi", 1)
        back = shift(chunk, "zhi", -1)
        far = shift(ahead, "zhi", 1) if part == 0 else shift(back, "zhi", -1)
        pieces += [chunk, ahead, back, far]

    acts = []
    for offset in (0, heads - 1, 1, 2):
        start = lax.rem(head + offset, heads) * group
        mine = lax.dynamic_slice_in_dim(activations, start, group, 0)
        theirs = lax.dynamic_slice_in_dim(other_act, start, group, 0)
        acts.append(jnp.concatenate([mine, theirs], axis=0))

    cov_sent = cov_partial(after(chunks[0], other_act), chunks[1], activations, inv_tokens, sites)
    cov_got = plane_exchange(cov_sent)
    cov = jnp.sum(cov_got.astype(F32), axis=0)

    def split(value, axis, index):
        place = lax.axis_index(axis)
        kept = lax.dynamic_index_in_dim(value, place, index, False)
        return kept, lax.dynamic_index_in_dim(value, 1 - place, index, False)

    grad_kept, grad_given = split(cov[:2], "zlo", 0)
    act_kept, act_given = split(cov[2].reshape(2, rows // 2, width), "zlo", 0)
    taken = shift(jnp.concatenate([grad_given, act_given], axis=0), "zlo", 1)
    grad_part = (grad_kept + taken[:rows]).reshape(heads, rows // heads, width)
    act_kept, act_given = split((act_kept + taken[rows:]).reshape(2, rows // 4, width), "core", 0)
    grad_rows = lax.dynamic_index_in_dim(grad_part, head, 0, False)
    for step in range(1, heads):
        given = lax.dynamic_index_in_dim(grad_part, lax.rem(head + step, heads), 0, False)
        grad_rows = grad_rows + shift(given, "zhi", step)
    act_rows = act_kept + swap_core(act_given)
    act_perm, grad_perm = [], []
    for zl in range(zlo_count):
        for site in range(sites):
            for co in range(2):
                source = (zl * sites + site) * 2 + co
                act_perm.append((source, (site * zlo_count + zl) * 2 + co))
                grad_perm.append((source, (co * 2 + zl) * sites + site))

    early = early_partial(pieces[:3] + pieces[4:7], acts[:3], inv_tokens)
    got = plane_exchange(weight_partial(early, pieces[3], pieces[7], acts[3], inv_tokens, sites))
    got = after(got, act_rows, grad_rows)
    share = jnp.sum(got.astype(F32), axis=0)
    mixed = lax.dot_general(
        share + shift(share, "zlo", 1),
        act_inverse.astype(F32),
        (((1,), (1,)), ((), ())),
        precision=lax.Precision.HIGHEST,
    ).astype(BF16)
    copies = jnp.broadcast_to(mixed[None], (sites, 2 * rows, width))
    mine = plane_exchange(copies).reshape(half, width)
    act_rows = lax.ppermute(act_rows, DP, act_perm)
    grad_rows = lax.ppermute(grad_rows, DP, grad_perm)

    mine = after(mine, act_rows, grad_rows)
    theirs = swap_core(mine)
    order = core.astype(jnp.int32).reshape(1)
    out_mine, sq_mine = right_product(order, mine, grad_inverse)
    out_theirs, sq_theirs = right_product(1 - order, theirs, grad_inverse)

    own_sq = sq_mine + sq_theirs
    sums = [own_sq] + [shift(own_sq, "zhi", step) for step in range(1, heads)]
    count = width * heads * out_width
    update, act_cov, grad_cov = final_update(order, sums, (act_rows, grad_rows), (out_mine, out_theirs), count)
    return (act_cov, grad_cov, update)


def solution(mesh):
    fine = Mesh(mesh.devices.reshape(2, 4, 4, 2, 4), EVERY)
    return jax.shard_map(
        body,
        mesh=fine,
        in_specs=(P(DP, "zhi"), P(EVERY, None), P("zhi", None), P()),
        out_specs=(P(("zhi",) + DP, None), P(EVERY, None), P("zhi", None)),
        check_vma=False,
    )
```

```python
import functools

import jax
import jax.numpy as jnp
from jax import lax
from jax.experimental import pallas as pl
from jax.experimental.pallas import tpu as pltpu
from jax.sharding import Mesh, PartitionSpec as P

DP = ("zlo", "x", "y", "core")
EVERY = DP + ("zhi",)
PLANE = ("x", "y")
BF16 = jnp.bfloat16
F32 = jnp.float32
LIMIT_MB = 16
LIMIT = pltpu.CompilerParams(vmem_limit_bytes=LIMIT_MB * 1024 * 1024)
VMEM = pl.BlockSpec(memory_space=pltpu.VMEM)
SMEM = pl.BlockSpec(memory_space=pltpu.SMEM)


def shift(value, axis, step):
    count = lax.axis_size(axis)
    return lax.ppermute(value, axis, [(i, (i + step) % count) for i in range(count)])


def after(value, *earlier):
    return lax.optimization_barrier((value,) + earlier)[0]


def token_dot(lhs, rhs):
    return lax.dot_general(lhs, rhs, (((0,), (0,)), ((), ())), preferred_element_type=F32)


def cost(flops, mib):
    return pl.CostEstimate(flops=flops, bytes_accessed=mib * 2**20, transcendentals=0)


def early_kernel(scale, *refs):
    pieces, acts, out = refs[:6], refs[6:9], refs[9]
    for part in range(2):
        total = sum(token_dot(pieces[3 * part + k][...], acts[k][...]) for k in range(3))
        out[part] = total * scale


def early_partial(pieces, acts, scale):
    width = acts[0].shape[1]
    return pl.pallas_call(
        functools.partial(early_kernel, scale),
        out_shape=jax.ShapeDtypeStruct((2, width, width), F32),
        in_specs=[VMEM] * 9,
        out_specs=VMEM,
        compiler_params=LIMIT,
        cost_estimate=cost(3 * 1024 * width * width, 6),
        name="early_partial",
    )(*pieces, *acts)


def weight_kernel(scale, early, first, second, act, out):
    rows = out.shape[1]
    for part, piece in enumerate((first, second)):
        total = early[part] + token_dot(piece[...], act[...]) * scale
        count = total.shape[0] // rows
        for index in range(count):
            out[part * count + index] = total[index * rows : (index + 1) * rows].astype(BF16)


def weight_partial(early, first, second, act, scale, sites):
    width = act.shape[1]
    return pl.pallas_call(
        functools.partial(weight_kernel, scale),
        out_shape=jax.ShapeDtypeStruct((sites, 2 * width // sites, width), BF16),
        in_specs=[VMEM] * 4,
        out_specs=VMEM,
        compiler_params=LIMIT,
        cost_estimate=cost(12 * 1024 * width * width, 6),
        name="weight_partial",
    )(early, first, second, act)


def cov_kernel(scale, first, second, acts, out):
    rows = out.shape[2]
    for slab, tokens in enumerate((first, second, acts)):
        value = tokens[...]
        total = token_dot(value, value)
        for index in range(out.shape[0]):
            out[index, slab] = (total[index * rows : (index + 1) * rows] * scale).astype(BF16)


def cov_partial(first, second, acts, scale, sites):
    width = acts.shape[1]
    return pl.pallas_call(
        functools.partial(cov_kernel, scale),
        out_shape=jax.ShapeDtypeStruct((sites, 3, width // sites, width), BF16),
        in_specs=[VMEM] * 3,
        out_specs=VMEM,
        compiler_params=LIMIT,
        cost_estimate=cost(2 * 1024 * width * width, 5),
        name="cov_partial",
    )(first, second, acts)


def right_kernel(half_index, left, inverse, out, squares):
    width = left.shape[1]
    total = 0.0
    for part in range(2):
        start = pl.multiple_of((2 * half_index[0] + part) * width, width)
        result = token_dot(left[part * width : (part + 1) * width, :], inverse[pl.ds(start, width), :])
        out[part] = result
        total = total + jnp.sum(result * result)
    squares[...] = jnp.broadcast_to(total, squares.shape)


def right_product(half_index, left, inverse):
    width = left.shape[1]
    return pl.pallas_call(
        right_kernel,
        out_shape=(jax.ShapeDtypeStruct((2, width, width), F32), jax.ShapeDtypeStruct((8, 128), F32)),
        in_specs=[SMEM, VMEM, VMEM],
        out_specs=(VMEM, VMEM),
        compiler_params=LIMIT,
        cost_estimate=cost(4 * width**3, 6),
        name="right_product",
    )(half_index, left, inverse)


def final_kernel(count, core, own, sq_a, sq_b, sq_c, act_rows, grad_rows, mine, theirs, out, act_out, grad_out):
    total = own[...] + sq_a[...] + sq_b[...] + sq_c[...]
    scale = lax.rsqrt(total / count + 1e-06)[0:1, 0:1]
    width = mine.shape[2]
    rows = out.shape[0]
    place = pl.ds(pl.multiple_of(pl.program_id(0) * rows, rows), rows)
    act_out[...] = act_rows[...]
    grad_out[...] = grad_rows[...]

    def write(first, second):
        for index in range(4):
            block = (first, second)[index // 2][index % 2, place]
            out[:, index * width : (index + 1) * width] = (block * scale).astype(BF16)

    @pl.when(core[0] == 0)
    def _():
        write(mine, theirs)

    @pl.when(core[0] != 0)
    def _():
        write(theirs, mine)


def final_update(core, sums, cov_rows, blocks, count):
    width = blocks[0].shape[1]
    rows = width // 5
    small = pl.BlockSpec((8, 128), lambda i: (0, 0))
    cov = pl.BlockSpec(cov_rows[0].shape, lambda i: (0, 0))
    cov_type = jax.ShapeDtypeStruct(cov_rows[0].shape, F32)
    return pl.pallas_call(
        functools.partial(final_kernel, count),
        grid=(5,),
        out_shape=(jax.ShapeDtypeStruct((width, 4 * width), BF16), cov_type, cov_type),
        in_specs=[SMEM] + [small] * 4 + [cov] * 2 + [VMEM] * 2,
        out_specs=(pl.BlockSpec((rows, 4 * width), lambda i: (i, 0)), cov, cov),
        compiler_params=LIMIT,
        cost_estimate=cost(4 * width * width, 10),
        name="final_update",
    )(core, *sums, *cov_rows, *blocks)


def plane_exchange(value):
    return lax.all_to_all(value, PLANE, split_axis=0, concat_axis=0, tiled=True)


def body(activations, output_grad, act_inverse, grad_inverse):
    token_count, width = activations.shape
    out_width = output_grad.shape[1]
    zlo_count = lax.axis_size("zlo")
    heads = lax.axis_size("zhi")
    sites = lax.axis_size("x") * lax.axis_size("y")
    dp_count = zlo_count * sites * 2
    group = token_count // heads
    half = out_width // 2
    rows = width // sites
    inv_tokens = 1.0 / (token_count * dp_count)
    core = lax.axis_index("core")
    head = lax.axis_index("zhi")

    def swap_core(value):
        return shift(value, "core", 1)

    chunks = []
    for part in range(2):
        kept = lax.dynamic_slice_in_dim(output_grad, core * half + part * width, width, 1)
        given = lax.dynamic_slice_in_dim(output_grad, (1 - core) * half + part * width, width, 1)
        chunks.append(jnp.concatenate([kept, swap_core(given)], axis=0))

    other_act = swap_core(activations)
    pieces = []
    for part, chunk in enumerate(chunks):
        ahead = shift(chunk, "zhi", 1)
        back = shift(chunk, "zhi", -1)
        far = shift(ahead, "zhi", 1) if part == 0 else shift(back, "zhi", -1)
        pieces += [chunk, ahead, back, far]

    acts = []
    for offset in (0, heads - 1, 1, 2):
        start = lax.rem(head + offset, heads) * group
        mine = lax.dynamic_slice_in_dim(activations, start, group, 0)
        theirs = lax.dynamic_slice_in_dim(other_act, start, group, 0)
        acts.append(jnp.concatenate([mine, theirs], axis=0))

    cov_sent = cov_partial(after(chunks[0], other_act), chunks[1], activations, inv_tokens, sites)
    cov_got = plane_exchange(cov_sent)
    cov = jnp.sum(cov_got.astype(F32), axis=0)

    def split(value, axis, index):
        place = lax.axis_index(axis)
        kept = lax.dynamic_index_in_dim(value, place, index, False)
        return kept, lax.dynamic_index_in_dim(value, 1 - place, index, False)

    grad_kept, grad_given = split(cov[:2], "zlo", 0)
    act_kept, act_given = split(cov[2].reshape(2, rows // 2, width), "zlo", 0)
    taken = shift(jnp.concatenate([grad_given, act_given], axis=0), "zlo", 1)
    grad_part = (grad_kept + taken[:rows]).reshape(heads, rows // heads, width)
    act_kept, act_given = split((act_kept + taken[rows:]).reshape(2, rows // 4, width), "core", 0)
    grad_rows = lax.dynamic_index_in_dim(grad_part, head, 0, False)
    for step in range(1, heads):
        given = lax.dynamic_index_in_dim(grad_part, lax.rem(head + step, heads), 0, False)
        grad_rows = grad_rows + shift(given, "zhi", step)
    act_rows = act_kept + swap_core(act_given)
    act_perm, grad_perm = [], []
    for zl in range(zlo_count):
        for site in range(sites):
            for co in range(2):
                source = (zl * sites + site) * 2 + co
                act_perm.append((source, (site * zlo_count + zl) * 2 + co))
                grad_perm.append((source, (co * 2 + zl) * sites + site))

    early = early_partial(pieces[:3] + pieces[4:7], acts[:3], inv_tokens)
    partial = weight_partial(early, pieces[3], pieces[7], acts[3], inv_tokens, sites)
    got = plane_exchange(after(partial, cov_got))
    got = after(got, taken)
    share = jnp.sum(got.astype(F32), axis=0)
    mixed = lax.dot_general(
        share + shift(share, "zlo", 1),
        act_inverse.astype(F32),
        (((1,), (1,)), ((), ())),
        precision=lax.Precision.HIGHEST,
    ).astype(BF16)
    copies = jnp.broadcast_to(mixed[None], (sites, 2 * rows, width))
    mine = plane_exchange(copies).reshape(half, width)
    act_rows = lax.ppermute(act_rows, DP, act_perm)
    grad_rows = lax.ppermute(grad_rows, DP, grad_perm)

    mine = after(mine, act_rows, grad_rows)
    theirs = swap_core(mine)
    order = core.astype(jnp.int32).reshape(1)
    out_mine, sq_mine = right_product(order, mine, grad_inverse)
    out_theirs, sq_theirs = right_product(1 - order, theirs, grad_inverse)

    own_sq = sq_mine + sq_theirs
    sums = [own_sq] + [shift(own_sq, "zhi", step) for step in range(1, heads)]
    count = width * heads * out_width
    update, act_cov, grad_cov = final_update(order, sums, (act_rows, grad_rows), (out_mine, out_theirs), count)
    return (act_cov, grad_cov, update)


def solution(mesh):
    fine = Mesh(mesh.devices.reshape(2, 4, 4, 2, 4), EVERY)
    return jax.shard_map(
        body,
        mesh=fine,
        in_specs=(P(DP, "zhi"), P(EVERY, None), P("zhi", None), P()),
        out_specs=(P(("zhi",) + DP, None), P(EVERY, None), P("zhi", None)),
        check_vma=False,
    )
```

```python
import functools

import jax
import jax.numpy as jnp
from jax import lax
from jax.experimental import pallas as pl
from jax.experimental.pallas import tpu as pltpu
from jax.sharding import Mesh, PartitionSpec as P

DP = ("zlo", "x", "y", "core")
EVERY = DP + ("zhi",)
PLANE = ("x", "y")
BF16 = jnp.bfloat16
F32 = jnp.float32
LIMIT_MB = 16
LIMIT = pltpu.CompilerParams(vmem_limit_bytes=LIMIT_MB * 1024 * 1024)
VMEM = pl.BlockSpec(memory_space=pltpu.VMEM)
SMEM = pl.BlockSpec(memory_space=pltpu.SMEM)


def shift(value, axis, step):
    count = lax.axis_size(axis)
    return lax.ppermute(value, axis, [(i, (i + step) % count) for i in range(count)])


def after(value, *earlier):
    return lax.optimization_barrier((value,) + earlier)[0]


def token_dot(lhs, rhs):
    return lax.dot_general(lhs, rhs, (((0,), (0,)), ((), ())), preferred_element_type=F32)


def cost(flops, mib):
    return pl.CostEstimate(flops=flops, bytes_accessed=mib * 2**20, transcendentals=0)


def early_kernel(scale, *refs):
    pieces, acts, out = refs[:6], refs[6:9], refs[9]
    for part in range(2):
        total = sum(token_dot(pieces[3 * part + k][...], acts[k][...]) for k in range(3))
        out[part] = total * scale


def early_partial(pieces, acts, scale):
    width = acts[0].shape[1]
    return pl.pallas_call(
        functools.partial(early_kernel, scale),
        out_shape=jax.ShapeDtypeStruct((2, width, width), F32),
        in_specs=[VMEM] * 9,
        out_specs=VMEM,
        compiler_params=LIMIT,
        cost_estimate=cost(3 * 1024 * width * width, 6),
        name="early_partial",
    )(*pieces, *acts)


def weight_kernel(scale, early, first, second, act, out):
    rows = out.shape[1]
    for part, piece in enumerate((first, second)):
        total = early[part] + token_dot(piece[...], act[...]) * scale
        count = total.shape[0] // rows
        for index in range(count):
            out[part * count + index] = total[index * rows : (index + 1) * rows].astype(BF16)


def weight_partial(early, first, second, act, scale, sites):
    width = act.shape[1]
    return pl.pallas_call(
        functools.partial(weight_kernel, scale),
        out_shape=jax.ShapeDtypeStruct((sites, 2 * width // sites, width), BF16),
        in_specs=[VMEM] * 4,
        out_specs=VMEM,
        compiler_params=LIMIT,
        cost_estimate=cost(12 * 1024 * width * width, 6),
        name="weight_partial",
    )(early, first, second, act)


def cov_kernel(scale, first, second, acts, out):
    rows = out.shape[2]
    for slab, tokens in enumerate((first, second, acts)):
        value = tokens[...]
        total = token_dot(value, value)
        for index in range(out.shape[0]):
            out[index, slab] = (total[index * rows : (index + 1) * rows] * scale).astype(BF16)


def cov_partial(first, second, acts, scale, sites):
    width = acts.shape[1]
    return pl.pallas_call(
        functools.partial(cov_kernel, scale),
        out_shape=jax.ShapeDtypeStruct((sites, 3, width // sites, width), BF16),
        in_specs=[VMEM] * 3,
        out_specs=VMEM,
        compiler_params=LIMIT,
        cost_estimate=cost(2 * 1024 * width * width, 5),
        name="cov_partial",
    )(first, second, acts)


def right_kernel(half_index, left, inverse, out, squares):
    width = left.shape[1]
    total = 0.0
    for part in range(2):
        start = pl.multiple_of((2 * half_index[0] + part) * width, width)
        result = token_dot(left[part * width : (part + 1) * width, :], inverse[pl.ds(start, width), :])
        out[part] = result
        total = total + jnp.sum(result * result)
    squares[...] = jnp.broadcast_to(total, squares.shape)


def right_product(half_index, left, inverse):
    width = left.shape[1]
    return pl.pallas_call(
        right_kernel,
        out_shape=(jax.ShapeDtypeStruct((2, width, width), F32), jax.ShapeDtypeStruct((8, 128), F32)),
        in_specs=[SMEM, VMEM, VMEM],
        out_specs=(VMEM, VMEM),
        compiler_params=LIMIT,
        cost_estimate=cost(4 * width**3, 6),
        name="right_product",
    )(half_index, left, inverse)


def final_kernel(count, core, own, sq_a, sq_b, sq_c, act_rows, grad_rows, mine, theirs, out, act_out, grad_out):
    total = own[...] + sq_a[...] + sq_b[...] + sq_c[...]
    scale = lax.rsqrt(total / count + 1e-06)[0:1, 0:1]
    width = mine.shape[2]
    rows = out.shape[0]
    place = pl.ds(pl.multiple_of(pl.program_id(0) * rows, rows), rows)
    act_out[...] = act_rows[...]
    grad_out[...] = grad_rows[...]

    def write(first, second):
        for index in range(4):
            block = (first, second)[index // 2][index % 2, place]
            out[:, index * width : (index + 1) * width] = (block * scale).astype(BF16)

    @pl.when(core[0] == 0)
    def _():
        write(mine, theirs)

    @pl.when(core[0] != 0)
    def _():
        write(theirs, mine)


def final_update(core, sums, cov_rows, blocks, count):
    width = blocks[0].shape[1]
    rows = width // 5
    small = pl.BlockSpec((8, 128), lambda i: (0, 0))
    cov = pl.BlockSpec(cov_rows[0].shape, lambda i: (0, 0))
    cov_type = jax.ShapeDtypeStruct(cov_rows[0].shape, F32)
    return pl.pallas_call(
        functools.partial(final_kernel, count),
        grid=(5,),
        out_shape=(jax.ShapeDtypeStruct((width, 4 * width), BF16), cov_type, cov_type),
        in_specs=[SMEM] + [small] * 4 + [cov] * 2 + [VMEM] * 2,
        out_specs=(pl.BlockSpec((rows, 4 * width), lambda i: (i, 0)), cov, cov),
        compiler_params=LIMIT,
        cost_estimate=cost(4 * width * width, 10),
        name="final_update",
    )(core, *sums, *cov_rows, *blocks)


def plane_exchange(value):
    return lax.all_to_all(value, PLANE, split_axis=0, concat_axis=0, tiled=True)


def body(activations, output_grad, act_inverse, grad_inverse):
    token_count, width = activations.shape
    out_width = output_grad.shape[1]
    zlo_count = lax.axis_size("zlo")
    heads = lax.axis_size("zhi")
    sites = lax.axis_size("x") * lax.axis_size("y")
    dp_count = zlo_count * sites * 2
    group = token_count // heads
    half = out_width // 2
    rows = width // sites
    inv_tokens = 1.0 / (token_count * dp_count)
    core = lax.axis_index("core")
    head = lax.axis_index("zhi")

    def swap_core(value):
        return shift(value, "core", 1)

    chunks = []
    for part in range(2):
        kept = lax.dynamic_slice_in_dim(output_grad, core * half + part * width, width, 1)
        given = lax.dynamic_slice_in_dim(output_grad, (1 - core) * half + part * width, width, 1)
        chunks.append(jnp.concatenate([kept, swap_core(given)], axis=0))

    other_act = swap_core(activations)
    pieces = []
    for part, chunk in enumerate(chunks):
        ahead = shift(chunk, "zhi", 1)
        back = shift(chunk, "zhi", -1)
        far = shift(ahead, "zhi", 1) if part == 0 else shift(back, "zhi", -1)
        pieces += [chunk, ahead, back, far]

    acts = []
    for offset in (0, heads - 1, 1, 2):
        start = lax.rem(head + offset, heads) * group
        mine = lax.dynamic_slice_in_dim(activations, start, group, 0)
        theirs = lax.dynamic_slice_in_dim(other_act, start, group, 0)
        acts.append(jnp.concatenate([mine, theirs], axis=0))

    cov_sent = cov_partial(after(chunks[0], other_act), chunks[1], activations, inv_tokens, sites)
    cov_got = plane_exchange(cov_sent)
    cov = jnp.sum(cov_got.astype(F32), axis=0)

    def split(value, axis, index):
        place = lax.axis_index(axis)
        kept = lax.dynamic_index_in_dim(value, place, index, False)
        return kept, lax.dynamic_index_in_dim(value, 1 - place, index, False)

    grad_kept, grad_given = split(cov[:2], "zlo", 0)
    act_kept, act_given = split(cov[2].reshape(2, rows // 2, width), "zlo", 0)
    taken = shift(jnp.concatenate([grad_given, act_given], axis=0), "zlo", 1)
    grad_part = (grad_kept + taken[:rows]).reshape(heads, rows // heads, width)
    act_kept, act_given = split((act_kept + taken[rows:]).reshape(2, rows // 4, width), "core", 0)
    grad_rows = lax.dynamic_index_in_dim(grad_part, head, 0, False)
    for step in range(1, heads):
        given = lax.dynamic_index_in_dim(grad_part, lax.rem(head + step, heads), 0, False)
        grad_rows = grad_rows + shift(given, "zhi", step)
    act_rows = act_kept + swap_core(act_given)
    act_perm, grad_perm = [], []
    for zl in range(zlo_count):
        for site in range(sites):
            for co in range(2):
                source = (zl * sites + site) * 2 + co
                act_perm.append((source, (site * zlo_count + zl) * 2 + co))
                grad_perm.append((source, (co * 2 + zl) * sites + site))

    early = early_partial(pieces[:3] + pieces[4:7], acts[:3], inv_tokens)
    partial = weight_partial(early, pieces[3], pieces[7], acts[3], inv_tokens, sites)
    got = plane_exchange(after(partial, cov_got))
    got = after(got, taken)
    share = jnp.sum(got.astype(F32), axis=0)
    mixed = lax.dot_general(
        share + shift(share, "zlo", 1),
        act_inverse.astype(F32),
        (((1,), (1,)), ((), ())),
        precision=lax.Precision.HIGHEST,
    ).astype(BF16)
    copies = jnp.broadcast_to(mixed[None], (sites, 2 * rows, width))
    mine = plane_exchange(copies).reshape(half, width)
    act_rows = lax.ppermute(act_rows, DP, act_perm)
    grad_rows = lax.ppermute(grad_rows, DP, grad_perm)

    theirs = swap_core(mine)
    order = core.astype(jnp.int32).reshape(1)
    out_mine, sq_mine = right_product(order, mine, grad_inverse)
    out_theirs, sq_theirs = right_product(1 - order, theirs, grad_inverse)

    own_sq = sq_mine + sq_theirs
    sums = [own_sq] + [shift(own_sq, "zhi", step) for step in range(1, heads)]
    count = width * heads * out_width
    update, act_cov, grad_cov = final_update(order, sums, (act_rows, grad_rows), (out_mine, out_theirs), count)
    return (act_cov, grad_cov, update)


def solution(mesh):
    fine = Mesh(mesh.devices.reshape(2, 4, 4, 2, 4), EVERY)
    return jax.shard_map(
        body,
        mesh=fine,
        in_specs=(P(DP, "zhi"), P(EVERY, None), P("zhi", None), P()),
        out_specs=(P(("zhi",) + DP, None), P(EVERY, None), P("zhi", None)),
        check_vma=False,
    )
```

```python
import functools

import jax
import jax.numpy as jnp
from jax import lax
from jax.experimental import pallas as pl
from jax.experimental.pallas import tpu as pltpu
from jax.sharding import Mesh, PartitionSpec as P

DP = ("zlo", "x", "y", "core")
EVERY = DP + ("zhi",)
PLANE = ("x", "y")
BF16 = jnp.bfloat16
F32 = jnp.float32
LIMIT_MB = 16
LIMIT = pltpu.CompilerParams(vmem_limit_bytes=LIMIT_MB * 1024 * 1024)
VMEM = pl.BlockSpec(memory_space=pltpu.VMEM)
SMEM = pl.BlockSpec(memory_space=pltpu.SMEM)


def shift(value, axis, step):
    count = lax.axis_size(axis)
    return lax.ppermute(value, axis, [(i, (i + step) % count) for i in range(count)])


def after(value, *earlier):
    return lax.optimization_barrier((value,) + earlier)[0]


def token_dot(lhs, rhs):
    return lax.dot_general(lhs, rhs, (((0,), (0,)), ((), ())), preferred_element_type=F32)


def cost(flops, mib):
    return pl.CostEstimate(flops=flops, bytes_accessed=mib * 2**20, transcendentals=0)


def early_kernel(scale, *refs):
    pieces, acts, out = refs[:6], refs[6:9], refs[9]
    for part in range(2):
        total = sum(token_dot(pieces[3 * part + k][...], acts[k][...]) for k in range(3))
        out[part] = total * scale


def early_partial(pieces, acts, scale):
    width = acts[0].shape[1]
    return pl.pallas_call(
        functools.partial(early_kernel, scale),
        out_shape=jax.ShapeDtypeStruct((2, width, width), F32),
        in_specs=[VMEM] * 9,
        out_specs=VMEM,
        compiler_params=LIMIT,
        cost_estimate=cost(3 * 1024 * width * width, 6),
        name="early_partial",
    )(*pieces, *acts)


def weight_kernel(scale, early, first, second, act, out):
    rows = out.shape[1]
    for part, piece in enumerate((first, second)):
        total = early[part] + token_dot(piece[...], act[...]) * scale
        count = total.shape[0] // rows
        for index in range(count):
            out[part * count + index] = total[index * rows : (index + 1) * rows].astype(BF16)


def weight_partial(early, first, second, act, scale, sites):
    width = act.shape[1]
    return pl.pallas_call(
        functools.partial(weight_kernel, scale),
        out_shape=jax.ShapeDtypeStruct((sites, 2 * width // sites, width), BF16),
        in_specs=[VMEM] * 4,
        out_specs=VMEM,
        compiler_params=LIMIT,
        cost_estimate=cost(12 * 1024 * width * width, 6),
        name="weight_partial",
    )(early, first, second, act)


def cov_kernel(scale, first, second, acts, out):
    rows = out.shape[2]
    for slab, tokens in enumerate((first, second, acts)):
        value = tokens[...]
        total = token_dot(value, value)
        for index in range(out.shape[0]):
            out[index, slab] = (total[index * rows : (index + 1) * rows] * scale).astype(BF16)


def cov_partial(first, second, acts, scale, sites):
    width = acts.shape[1]
    return pl.pallas_call(
        functools.partial(cov_kernel, scale),
        out_shape=jax.ShapeDtypeStruct((sites, 3, width // sites, width), BF16),
        in_specs=[VMEM] * 3,
        out_specs=VMEM,
        compiler_params=LIMIT,
        cost_estimate=cost(2 * 1024 * width * width, 5),
        name="cov_partial",
    )(first, second, acts)


def right_kernel(half_index, left, inverse, out, squares):
    width = left.shape[1]
    total = 0.0
    for part in range(2):
        start = pl.multiple_of((2 * half_index[0] + part) * width, width)
        result = token_dot(left[part * width : (part + 1) * width, :], inverse[pl.ds(start, width), :])
        out[part] = result
        total = total + jnp.sum(result * result)
    squares[...] = jnp.broadcast_to(total, squares.shape)


def right_product(half_index, left, inverse):
    width = left.shape[1]
    return pl.pallas_call(
        right_kernel,
        out_shape=(jax.ShapeDtypeStruct((2, width, width), F32), jax.ShapeDtypeStruct((8, 128), F32)),
        in_specs=[SMEM, VMEM, VMEM],
        out_specs=(VMEM, VMEM),
        compiler_params=LIMIT,
        cost_estimate=cost(4 * width**3, 6),
        name="right_product",
    )(half_index, left, inverse)


def final_kernel(count, core, own, sq_a, sq_b, sq_c, act_rows, grad_rows, mine, theirs, out, act_out, grad_out):
    total = own[...] + sq_a[...] + sq_b[...] + sq_c[...]
    scale = lax.rsqrt(total / count + 1e-06)[0:1, 0:1]
    width = mine.shape[2]
    rows = out.shape[0]
    place = pl.ds(pl.multiple_of(pl.program_id(0) * rows, rows), rows)
    act_out[...] = act_rows[...]
    grad_out[...] = grad_rows[...]

    def write(first, second):
        for index in range(4):
            block = (first, second)[index // 2][index % 2, place]
            out[:, index * width : (index + 1) * width] = (block * scale).astype(BF16)

    @pl.when(core[0] == 0)
    def _():
        write(mine, theirs)

    @pl.when(core[0] != 0)
    def _():
        write(theirs, mine)


def final_update(core, sums, cov_rows, blocks, count):
    width = blocks[0].shape[1]
    rows = width // 5
    small = pl.BlockSpec((8, 128), lambda i: (0, 0))
    cov = pl.BlockSpec(cov_rows[0].shape, lambda i: (0, 0))
    cov_type = jax.ShapeDtypeStruct(cov_rows[0].shape, F32)
    return pl.pallas_call(
        functools.partial(final_kernel, count),
        grid=(5,),
        out_shape=(jax.ShapeDtypeStruct((width, 4 * width), BF16), cov_type, cov_type),
        in_specs=[SMEM] + [small] * 4 + [cov] * 2 + [VMEM] * 2,
        out_specs=(pl.BlockSpec((rows, 4 * width), lambda i: (i, 0)), cov, cov),
        compiler_params=LIMIT,
        cost_estimate=cost(4 * width * width, 10),
        name="final_update",
    )(core, *sums, *cov_rows, *blocks)


def plane_exchange(value):
    return lax.all_to_all(value, PLANE, split_axis=0, concat_axis=0, tiled=True)


def body(activations, output_grad, act_inverse, grad_inverse):
    token_count, width = activations.shape
    out_width = output_grad.shape[1]
    zlo_count = lax.axis_size("zlo")
    heads = lax.axis_size("zhi")
    sites = lax.axis_size("x") * lax.axis_size("y")
    dp_count = zlo_count * sites * 2
    group = token_count // heads
    half = out_width // 2
    rows = width // sites
    inv_tokens = 1.0 / (token_count * dp_count)
    core = lax.axis_index("core")
    head = lax.axis_index("zhi")

    def swap_core(value):
        return shift(value, "core", 1)

    chunks = []
    for part in range(2):
        kept = lax.dynamic_slice_in_dim(output_grad, core * half + part * width, width, 1)
        given = lax.dynamic_slice_in_dim(output_grad, (1 - core) * half + part * width, width, 1)
        chunks.append(jnp.concatenate([kept, swap_core(given)], axis=0))

    other_act = swap_core(activations)
    pieces = []
    for part, chunk in enumerate(chunks):
        ahead = shift(chunk, "zhi", 1)
        back = shift(chunk, "zhi", -1)
        far = shift(ahead, "zhi", 1) if part == 0 else shift(back, "zhi", -1)
        pieces += [chunk, ahead, back, far]

    acts = []
    for offset in (0, heads - 1, 1, 2):
        start = lax.rem(head + offset, heads) * group
        mine = lax.dynamic_slice_in_dim(activations, start, group, 0)
        theirs = lax.dynamic_slice_in_dim(other_act, start, group, 0)
        acts.append(jnp.concatenate([mine, theirs], axis=0))

    cov_sent = cov_partial(after(chunks[0], other_act), chunks[1], activations, inv_tokens, sites)
    cov_got = plane_exchange(cov_sent)
    cov = jnp.sum(cov_got.astype(F32), axis=0)

    def split(value, axis, index):
        place = lax.axis_index(axis)
        kept = lax.dynamic_index_in_dim(value, place, index, False)
        return kept, lax.dynamic_index_in_dim(value, 1 - place, index, False)

    grad_kept, grad_given = split(cov[:2], "zlo", 0)
    act_kept, act_given = split(cov[2].reshape(2, rows // 2, width), "zlo", 0)
    taken = shift(jnp.concatenate([grad_given, act_given], axis=0), "zlo", 1)
    grad_part = (grad_kept + taken[:rows]).reshape(heads, rows // heads, width)
    act_kept, act_given = split((act_kept + taken[rows:]).reshape(2, rows // 4, width), "core", 0)
    grad_rows = lax.dynamic_index_in_dim(grad_part, head, 0, False)
    for step in range(1, heads):
        given = lax.dynamic_index_in_dim(grad_part, lax.rem(head + step, heads), 0, False)
        grad_rows = grad_rows + shift(given, "zhi", step)
    act_rows = act_kept + swap_core(act_given)
    act_perm, grad_perm = [], []
    for zl in range(zlo_count):
        for site in range(sites):
            for co in range(2):
                source = (zl * sites + site) * 2 + co
                act_perm.append((source, (site * zlo_count + zl) * 2 + co))
                grad_perm.append((source, (co * 2 + zl) * sites + site))

    early = early_partial(pieces[:3] + pieces[4:7], acts[:3], inv_tokens)
    partial = weight_partial(early, pieces[3], pieces[7], acts[3], inv_tokens, sites)
    got = plane_exchange(after(partial, cov_got))
    got = after(got, taken)
    share = jnp.sum(got.astype(F32), axis=0)
    mixed = lax.dot_general(
        share + shift(share, "zlo", 1),
        act_inverse.astype(F32),
        (((1,), (1,)), ((), ())),
        precision=lax.Precision.HIGHEST,
    ).astype(BF16)
    copies = jnp.broadcast_to(mixed[None], (sites, 2 * rows, width))
    mine = plane_exchange(copies).reshape(half, width)
    summed_rows = (act_rows, grad_rows)
    act_rows = lax.ppermute(act_rows, DP, act_perm)
    grad_rows = lax.ppermute(grad_rows, DP, grad_perm)

    mine = after(mine, *summed_rows)
    theirs = swap_core(mine)
    order = core.astype(jnp.int32).reshape(1)
    out_mine, sq_mine = right_product(order, mine, grad_inverse)
    out_theirs, sq_theirs = right_product(1 - order, theirs, grad_inverse)

    own_sq = sq_mine + sq_theirs
    sums = [own_sq] + [shift(own_sq, "zhi", step) for step in range(1, heads)]
    count = width * heads * out_width
    update, act_cov, grad_cov = final_update(order, sums, (act_rows, grad_rows), (out_mine, out_theirs), count)
    return (act_cov, grad_cov, update)


def solution(mesh):
    fine = Mesh(mesh.devices.reshape(2, 4, 4, 2, 4), EVERY)
    return jax.shard_map(
        body,
        mesh=fine,
        in_specs=(P(DP, "zhi"), P(EVERY, None), P("zhi", None), P()),
        out_specs=(P(("zhi",) + DP, None), P(EVERY, None), P("zhi", None)),
        check_vma=False,
    )
```
